32 devices in a mesh: ctx: 4 (over x, core), head: 8 (over z, y).
Axes of the slice: x: 2, y: 2, z: 4, core: 2. Of those that a mesh axis runs over, the one named last changes fastest.
Arguments:
- queries: bfloat16 [8192, 8192], P(('ctx', 'head')), may hold values from -30 to 30
- keys: bfloat16 [8192, 8192], P(('ctx', 'head')), may hold values from -30 to 30
- values: bfloat16 [8192, 8192], P(('ctx', 'head')), may hold values from -6 to 6
- rates: bfloat16 [8192, 32], P(('ctx', 'head')), may hold values from 0.0009994507 to 0.0099487305
- fast_init: bfloat16 [3, 32, 256, 256], P(None, 'head'), may hold values from -0.375 to 0.375
- gain: float32 [8192], replicated, may hold values from 0.25 to 1.75
Outputs:
- mixed: bfloat16 [8192, 8192], P(('ctx', 'head'))
The draws below stay inside these ranges and needn't reach their ends.
All inputs are finite; a program needn't handle non-finite values.
Results may differ from the reference program's by a relative error of at most 0.0095.
Values may be sent and summed in bfloat16 or wider, within the bound.
No kernel may reach another device: no remote copies, remote signals or barrier semaphores. Data moves between devices by JAX's collectives and lax.ppermute only.
A program may use at most 192 MiB of HBM per device.

```python
import math
import jax
import jax.numpy as jnp
from jax import lax

HEADS = 32
HD = 256
HID = 256
WINDOW = 2048
D = 8192
GROUP = 2048
TOKENS = 8192


def draw_pair(key):
    base = jax.random.fold_in(key, 4242)
    key_first, key_second = jax.random.split(base)
    query_vals = jnp.clip(jax.random.normal(key_first, (TOKENS, D), jnp.float32), -6.0, 6.0)
    key_vals = jnp.clip(jax.random.normal(key_second, (TOKENS, D), jnp.float32), -6.0, 6.0)
    return (query_vals, key_vals)


def draw_queries(key, part):
    return draw_pair(key)[0].astype(jnp.bfloat16)


def draw_keys(key, part):
    return draw_pair(key)[1].astype(jnp.bfloat16)


def shard_levels(stream_key, extent, pieces, smallest, largest):
    def one(dim, blocks):
        steps = jax.random.uniform(jax.random.fold_in(jax.random.fold_in(stream_key, 6), dim), (blocks,), jnp.float32, smallest / len(pieces), largest / len(pieces))
        return jnp.repeat(jnp.exp(steps), extent[dim] // blocks).reshape((-1,) + (1,) * (len(extent) - dim - 1))

    loudness = one(*pieces[0])
    for cut in pieces[1:]:
        loudness = loudness * one(*cut)
    return loudness


def scatter_about(key, extent, scale, bound, pieces=(), kind=jnp.bfloat16):
    level = shard_levels(key, extent, pieces, -0.22, 0.18) if pieces else 1.0
    array = jax.random.normal(key, extent, jnp.float32) * scale * level
    return jnp.minimum(jnp.maximum(array, -bound), bound).astype(kind)


def setup_inputs(seed: int = 0) -> dict:
    splits = jax.random.split(jax.random.key(seed), 7)
    return {
        "queries": draw_queries(jax.random.fold_in(splits[6], 71), 0),
        "keys": draw_keys(jax.random.fold_in(splits[6], 71), 0),
        "values": scatter_about(splits[2], (TOKENS, D), 1.0, 6.0, ((0, 32),)),
        "rates": jnp.clip(jnp.exp(math.log(0.0099487305) - 2.2979944 * jax.random.uniform(splits[3], (TOKENS, HEADS), jnp.float32) ** shard_levels(splits[3], (TOKENS, HEADS), ((0, 32),), -0.2, 0.2)), 0.0009994507, 0.0099487305).astype(jnp.bfloat16),
        "fast_init": scatter_about(splits[4], (3, HEADS, HID, HD), HD ** -0.5, 0.375, ((1, 8),)),
        "gain": jnp.clip(1.0 + 0.15 * jax.random.normal(splits[5], (D,), jnp.float32), 0.25, 1.75),
    }


EPSILON = 1e-06

def silu_parts(pre):
    sigma = jax.nn.sigmoid(pre)
    return (pre * sigma, sigma)

def attention_head(query_head, key_head, value_head):
    block = min(512, TOKENS)
    scale = HD ** (-0.5)
    key_pad = jnp.concatenate([jnp.zeros((WINDOW, HD), jnp.bfloat16), key_head], 0)
    value_pad = jnp.concatenate([jnp.zeros((WINDOW, HD), jnp.bfloat16), value_head], 0)

    def attend(number):
        start = number * block
        query_block = lax.dynamic_slice_in_dim(query_head, start, block, 0)
        key_block = lax.dynamic_slice_in_dim(key_pad, start, block + WINDOW, 0)
        value_block = lax.dynamic_slice_in_dim(value_pad, start, block + WINDOW, 0)
        scores = jnp.dot(query_block, key_block.T, preferred_element_type=jnp.float32) * scale
        query_pos = start + jnp.arange(block, dtype=jnp.int32)[:, None]
        key_pos = start - WINDOW + jnp.arange(block + WINDOW, dtype=jnp.int32)[None, :]
        valid = (key_pos <= query_pos) & (key_pos > query_pos - WINDOW) & (key_pos >= 0)
        masked = jnp.where(valid, scores, -jnp.inf)
        top = lax.optimization_barrier(jnp.max(masked, axis=1, keepdims=True))
        weights = jnp.where(valid, jnp.exp(masked - top), 0.0)
        probs = (weights / lax.optimization_barrier(jnp.sum(weights, axis=1, keepdims=True))).astype(jnp.bfloat16)
        return jnp.dot(probs, value_block, preferred_element_type=jnp.float32)
    parts = lax.map(attend, jnp.arange(TOKENS // block, dtype=jnp.int32))
    return parts.reshape(TOKENS, HD)

def group_update(group_keys, group_values, group_rates, weights):
    gate_pre = jnp.dot(group_keys, weights[0].T, preferred_element_type=jnp.float32)
    up_pre = jnp.dot(group_keys, weights[1].T, preferred_element_type=jnp.float32)
    gate_act, sigma = silu_parts(gate_pre)
    hidden = (gate_act * up_pre).astype(jnp.bfloat16)
    targets = (group_rates[:, None] * group_values.astype(jnp.float32)).astype(jnp.bfloat16)
    back = jnp.dot(targets, weights[2].T, preferred_element_type=jnp.float32)
    back_gate = (back * up_pre * sigma * (1.0 + gate_pre * (1.0 - sigma))).astype(jnp.bfloat16)
    back_up = (back * gate_act).astype(jnp.bfloat16)
    return jnp.stack([jnp.dot(back_gate.T, group_keys, preferred_element_type=jnp.float32), jnp.dot(back_up.T, group_keys, preferred_element_type=jnp.float32), jnp.dot(hidden.T, targets, preferred_element_type=jnp.float32)])

def apply_group(group_queries, prior, weights):
    initial = weights.astype(jnp.float32)
    target_ms = lax.optimization_barrier(jnp.mean(initial * initial, axis=-1, keepdims=True))
    renewed = initial + prior
    current = lax.optimization_barrier(jnp.mean(renewed * renewed, axis=-1, keepdims=True))
    fitted = (renewed * jnp.sqrt(target_ms) * lax.rsqrt(current + EPSILON)).astype(jnp.bfloat16)
    q_gate = jnp.dot(group_queries, fitted[0].T, preferred_element_type=jnp.float32)
    q_up = jnp.dot(group_queries, fitted[1].T, preferred_element_type=jnp.float32)
    q_hidden = (silu_parts(q_gate)[0] * q_up).astype(jnp.bfloat16)
    return jnp.dot(q_hidden, fitted[2], preferred_element_type=jnp.float32)

def reference(queries, keys, values, rates, fast_init, gain):
    count = TOKENS // GROUP

    def one_head(head):
        start = head * HD
        query_head = lax.dynamic_slice_in_dim(queries, start, HD, 1)
        key_head = lax.dynamic_slice_in_dim(keys, start, HD, 1)
        value_head = lax.dynamic_slice_in_dim(values, start, HD, 1)
        rate_head = lax.dynamic_slice_in_dim(rates, head, 1, 1)[:, 0].astype(jnp.float32)
        weights = lax.dynamic_index_in_dim(fast_init, head, 1, keepdims=False)
        attended = attention_head(query_head, key_head, value_head)
        updates = lax.map(lambda item: group_update(item[0], item[1], item[2], weights), (key_head.reshape(count, GROUP, HD), value_head.reshape(count, GROUP, HD), rate_head.reshape(count, GROUP)))
        running = jnp.cumsum(updates, axis=0)
        prior = jnp.concatenate([jnp.zeros((1,) + updates.shape[1:], jnp.float32), running[:-1]], 0)
        recalled = lax.map(lambda item: apply_group(item[0], item[1], weights), (query_head.reshape(count, GROUP, HD), prior))
        return attended + recalled.reshape(TOKENS, HD)
    combined = lax.map(one_head, jnp.arange(HEADS, dtype=jnp.int32))
    combined = jnp.transpose(combined, (1, 0, 2)).reshape(TOKENS, D)
    factor = lax.rsqrt(lax.optimization_barrier(jnp.mean(combined * combined, axis=1, keepdims=True)) + EPSILON)
    return (combined * factor * gain).astype(jnp.bfloat16)
```

```python
import functools

import jax
import jax.numpy as jnp
from jax import lax
from jax.experimental import pallas as pl
from jax.experimental.pallas import tpu as pltpu
from jax.sharding import PartitionSpec as P

WINDOW = 2048
EPSILON = 1e-06
LOG2E = 1.4426950408889634
NT = (((1,), (1,)), ((), ()))
SUBLANES = 16
PARAMS = pltpu.CompilerParams(vmem_limit_bytes=60 << 20)
COST = 0.001


def dot(a, b):
    return jnp.dot(a, b, preferred_element_type=jnp.float32)


def dot_nt(a, b):
    return lax.dot_general(a, b, NT, preferred_element_type=jnp.float32)


def cost(flops, bytes_accessed, transcendentals=0):
    return pl.CostEstimate(
        flops=int(flops * COST),
        bytes_accessed=int(bytes_accessed * COST),
        transcendentals=int(transcendentals * COST),
    )


def from_behind(value, axis, steps):
    count = lax.axis_size(axis)
    return lax.ppermute(value, axis, [(source, source + steps) for source in range(count - steps)])


def exchange(value):
    return lax.all_to_all(value, "head", split_axis=0, concat_axis=0, tiled=True)


def after(value, earlier):
    return lax.optimization_barrier((value, earlier))[0]


def pack_kernel(*refs, with_rates):
    *sources, out_ref = refs
    rows, size = sources[0].shape[0], out_ref.shape[2]
    at = 0
    if with_rates:
        rate_ref = sources.pop()
        heads = rate_ref.shape[0] // pl.num_programs(0)
        shape = (SUBLANES, rate_ref.shape[0])
        source = lax.broadcasted_iota(jnp.int32, shape, 1)
        target = lax.broadcasted_iota(jnp.int32, shape, 0) + pl.program_id(0) * heads
        chosen = dot((source == target).astype(jnp.bfloat16), rate_ref[...])
        end = out_ref.shape[1]
        out_ref[0, end - SUBLANES : end, :rows] = chosen.astype(jnp.bfloat16)
    for ref in sources:
        for h in range(ref.shape[1] // size):
            out_ref[0, at : at + rows] = ref[:, h * size : (h + 1) * size]
            at += rows


def pack(parts, peers, group, groups, size, rates=None):
    rows = parts[0][0].shape[0]
    specs = [
        pl.BlockSpec((rows, group * size), functools.partial(lambda d, g: (0, d * groups + g), g=g))
        for _, g in parts
    ]
    operands = [array for array, _ in parts]
    count = len(parts) * group * rows
    if rates is not None:
        operands.append(rates)
        specs.append(pl.BlockSpec(rates.shape, lambda d: (0, 0)))
        count += SUBLANES
    return pl.pallas_call(
        functools.partial(pack_kernel, with_rates=rates is not None),
        grid=(peers,),
        in_specs=specs,
        out_specs=pl.BlockSpec((1, count, size), lambda d: (d, 0, 0)),
        out_shape=jax.ShapeDtypeStruct((peers, count, size), jnp.bfloat16),
        compiler_params=PARAMS,
        cost_estimate=cost(0, 4 * peers * count * size),
    )(*operands)


def update_kernel(first_head, k_ref, v_ref, rate_ref, init_ref, out_ref):
    peers, rows, size = k_ref.shape
    head = first_head + pl.program_id(0)
    w_gate, w_up, w_down = init_ref[0, 0], init_ref[1, 0], init_ref[2, 0]
    span = max(1, 512 // rows)
    total = [0.0, 0.0, 0.0]
    for start in range(0, peers, span):
        here = slice(start, start + span)
        tokens = span * rows
        keys = k_ref[here].reshape(tokens, size)
        targets = []
        for s in range(start, start + span):
            turned = jnp.transpose(rate_ref[s].astype(jnp.float32))[:rows]
            lane = lax.broadcasted_iota(jnp.int32, turned.shape, 1)
            rate = jnp.sum(jnp.where(lane == head, turned, 0.0), axis=1, keepdims=True)
            targets.append((rate * v_ref[s].astype(jnp.float32)).astype(jnp.bfloat16))
        targets = jnp.concatenate(targets, axis=0)
        gate_pre = dot_nt(w_gate, keys)
        up_pre = dot_nt(w_up, keys)
        back = dot_nt(w_down, targets)
        sigma = jax.nn.sigmoid(gate_pre)
        gate_act = gate_pre * sigma
        hidden = (gate_act * up_pre).astype(jnp.bfloat16)
        back_gate = (back * up_pre * sigma * (1.0 + gate_pre * (1.0 - sigma))).astype(jnp.bfloat16)
        back_up = (back * gate_act).astype(jnp.bfloat16)
        total[0] += dot(back_gate, keys)
        total[1] += dot(back_up, keys)
        total[2] += dot(hidden, targets)
    for i in range(3):
        out_ref[i, 0] = total[i]


def updates(packed, k_at, v_at, rate_from, fast_init, first_head, group, rows):
    peers, depth, size = rate_from.shape
    hid = fast_init.shape[2]
    length = peers * rows
    block = (peers, rows, size)
    last = depth // SUBLANES - 1
    return pl.pallas_call(
        functools.partial(update_kernel, first_head),
        grid=(group,),
        in_specs=[
            pl.BlockSpec(block, lambda h: (0, k_at + h, 0)),
            pl.BlockSpec(block, lambda h: (0, v_at + h, 0)),
            pl.BlockSpec((peers, SUBLANES, size), lambda h: (0, last, 0)),
            pl.BlockSpec((3, 1, hid, size), lambda h: (0, first_head + h, 0, 0)),
        ],
        out_specs=pl.BlockSpec((3, 1, hid, size), lambda h: (0, h, 0, 0)),
        out_shape=jax.ShapeDtypeStruct((3, group, hid, size), jnp.float32),
        compiler_params=PARAMS,
        cost_estimate=cost(
            group * 6 * 2 * length * size * hid, group * 4 * length * size, group * length * hid
        ),
    )(packed, packed, rate_from, fast_init)


def attend_kernel(place_ref, q_ref, k_ref, v_ref, ek_ref, ev_ref, fit_ref, out_ref):
    peers, rows, size = q_ref.shape
    length = peers * rows
    first = place_ref[0] == 0
    factor = size**-0.5 * LOG2E
    tile = min(256, length)
    span = tile // rows
    flat = lambda ref, low, high: ref[low // rows : high // rows].reshape(high - low, size)
    row = lax.broadcasted_iota(jnp.int32, (tile, tile), 0)
    col = lax.broadcasted_iota(jnp.int32, (tile, tile), 1)
    f_gate, f_up, f_down = fit_ref[0, 0], fit_ref[1, 0], fit_ref[2, 0]
    for start in range(0, length, tile):
        stop = start + tile
        query = flat(q_ref, start, stop)
        far = dot_nt(query, flat(ek_ref, start, length))
        near = dot_nt(query, flat(k_ref, 0, stop))
        far_edge = jnp.where(col > row, far[:, :tile], -jnp.inf)
        near_edge = jnp.where(col <= row, near[:, start:], -jnp.inf)
        far_parts = [far_edge] + ([far[:, tile:]] if far.shape[1] > tile else [])
        near_parts = ([near[:, :start]] if start else []) + [near_edge]
        far = jnp.concatenate(far_parts, axis=1)
        near = jnp.concatenate(near_parts, axis=1)
        top_far = jnp.max(far, axis=1, keepdims=True)
        top_near = jnp.max(near, axis=1, keepdims=True)
        top = jnp.where(first, top_near, jnp.maximum(top_near, top_far))
        shift = top * factor
        shift_far = jnp.where(first, jnp.inf, shift)
        w_far = jnp.exp2(far * factor - shift_far)
        w_near = jnp.exp2(near * factor - shift)
        weight = jnp.sum(w_far, axis=1, keepdims=True) + jnp.sum(w_near, axis=1, keepdims=True)
        attended = dot(w_far.astype(jnp.bfloat16), flat(ev_ref, start, length))
        attended += dot(w_near.astype(jnp.bfloat16), flat(v_ref, 0, stop))
        q_gate = dot_nt(query, f_gate)
        q_up = dot_nt(query, f_up)
        q_hidden = (q_gate * jax.nn.sigmoid(q_gate) * q_up).astype(jnp.bfloat16)
        combined = attended / weight + dot(q_hidden, f_down)
        out_ref[start // rows : stop // rows, 0] = combined.astype(jnp.bfloat16).reshape(
            span, rows, size
        )


def attend(place, q_from, q_at, kv_from, k_at, v_at, edge, ek_at, ev_at, fitted, group, rows):
    peers, _, size = q_from.shape
    hid = fitted.shape[2]
    length = peers * rows
    at = lambda start: pl.BlockSpec((peers, rows, size), lambda h: (0, start + h, 0))
    return pl.pallas_call(
        attend_kernel,
        grid=(group,),
        in_specs=[
            pl.BlockSpec(memory_space=pltpu.SMEM),
            at(q_at),
            at(k_at),
            at(v_at),
            at(ek_at),
            at(ev_at),
            pl.BlockSpec((3, 1, hid, size), lambda h: (0, h, 0, 0)),
        ],
        out_specs=pl.BlockSpec((peers, 1, rows, size), lambda h: (0, h, 0, 0)),
        out_shape=jax.ShapeDtypeStruct((peers, group, rows, size), jnp.bfloat16),
        compiler_params=PARAMS,
        cost_estimate=cost(
            group * length * size * 2 * (2 * (WINDOW + 256) + 3 * hid),
            group * 12 * length * size,
            group * length * (WINDOW + 256),
        ),
    )(place, q_from, kv_from, kv_from, edge, edge, fitted)


def norm_kernel(*refs):
    *sources, gain_ref, out_ref = refs
    peers, group, rows, size = sources[0].shape
    heads = group * len(sources)
    width = out_ref.shape[1]
    square = jnp.zeros((rows, size), jnp.float32)
    for ref in sources:
        for s in range(peers):
            for h in range(group):
                x = ref[s, h].astype(jnp.float32)
                square += x * x
    factor = lax.rsqrt(jnp.sum(square, axis=1, keepdims=True) / width + EPSILON)
    for number, ref in enumerate(sources):
        for s in range(peers):
            for h in range(group):
                low = (s * heads + number * group + h) * size
                x = ref[s, h].astype(jnp.float32)
                out_ref[:, low : low + size] = (
                    x * factor * gain_ref[:, low : low + size]
                ).astype(jnp.bfloat16)


def normalize(parts, gain):
    peers, group, rows, size = parts[0].shape
    width = gain.shape[0]
    step = min(32, rows)
    return pl.pallas_call(
        norm_kernel,
        grid=(rows // step,),
        in_specs=[pl.BlockSpec((peers, group, step, size), lambda i: (0, 0, i, 0)) for _ in parts]
        + [pl.BlockSpec((1, width), lambda i: (0, 0))],
        out_specs=pl.BlockSpec((step, width), lambda i: (i, 0)),
        out_shape=jax.ShapeDtypeStruct((rows, width), jnp.bfloat16),
        compiler_params=PARAMS,
        cost_estimate=cost(5 * rows * width, 4 * rows * width),
    )(*parts, gain.reshape(1, width))


def earlier_sum(value, axis):
    count = lax.axis_size(axis)
    running, before, steps = value, jnp.zeros_like(value), 1
    while steps < count:
        arrived = from_behind(running.astype(jnp.bfloat16), axis, steps).astype(jnp.float32)
        before = before + arrived
        running = running + arrived
        steps *= 2
    return before


def refit(initial, before):
    initial = initial.astype(jnp.float32)
    target_ms = jnp.mean(initial * initial, axis=3, keepdims=True)
    renewed = initial + before
    current = jnp.mean(renewed * renewed, axis=3, keepdims=True)
    return (renewed * jnp.sqrt(target_ms) * lax.rsqrt(current + EPSILON)).astype(jnp.bfloat16)


def on_device(queries, keys, values, rates, fast_init, gain):
    peers = lax.axis_size("head")
    rows = queries.shape[0]
    heads = fast_init.shape[1]
    size = fast_init.shape[3]
    groups = 2
    group = heads // groups
    place = lax.axis_index("ctx").astype(jnp.int32).reshape(1)
    lay = lambda *parts, **more: pack(parts, peers, group, groups, size, **more)

    kv_a = exchange(lay((keys, 0), (values, 0), rates=rates.T))
    kv_a, kvq = lax.optimization_barrier((kv_a, lay((keys, 1), (values, 1), (queries, 0))))
    kvq = exchange(kvq)
    edge_a = from_behind(kv_a, "ctx", 1)
    up_a = updates(kv_a, 0, group, kv_a, fast_init, 0, group, rows)
    fit_a = refit(fast_init[:, :group], earlier_sum(up_a, "ctx"))
    kvq, q_b, fit_a = lax.optimization_barrier((kvq, lay((queries, 1)), fit_a))
    q_b = exchange(q_b)
    kv_b = kvq[:, : 2 * group * rows]
    edge_b = from_behind(kv_b, "ctx", 1)
    up_b = updates(kv_b, 0, group, kv_a, fast_init, group, group, rows)
    fit_b = refit(fast_init[:, group:], earlier_sum(up_b, "ctx"))
    fit_a = after(fit_a, up_b)
    out_a = attend(place, kvq, 2 * group, kv_a, 0, group, edge_a, 0, group, fit_a, group, rows)
    back_a = exchange(after(out_a, q_b))
    out_b = attend(place, q_b, 0, kv_b, 0, group, edge_b, 0, group, fit_b, group, rows)
    back_b = exchange(after(out_b, back_a))
    return normalize([back_a, back_b], gain)


def solution(mesh):
    rows = P(("ctx", "head"), None)
    in_specs = (rows, rows, rows, rows, P(None, "head", None, None), P())
    return jax.shard_map(on_device, mesh=mesh, in_specs=in_specs, out_specs=rows, check_vma=False)
```

```python
import functools

import jax
import jax.numpy as jnp
from jax import lax
from jax.experimental import pallas as pl
from jax.experimental.pallas import tpu as pltpu
from jax.sharding import PartitionSpec as P

WINDOW = 2048
EPSILON = 1e-06
LOG2E = 1.4426950408889634
NT = (((1,), (1,)), ((), ()))
SUBLANES = 16
PARAMS = pltpu.CompilerParams(vmem_limit_bytes=60 << 20)
COST = 0.001


def dot(a, b):
    return jnp.dot(a, b, preferred_element_type=jnp.float32)


def dot_nt(a, b):
    return lax.dot_general(a, b, NT, preferred_element_type=jnp.float32)


def cost(flops, bytes_accessed, transcendentals=0):
    return pl.CostEstimate(
        flops=int(flops * COST),
        bytes_accessed=int(bytes_accessed * COST),
        transcendentals=int(transcendentals * COST),
    )


def from_behind(value, axis, steps):
    count = lax.axis_size(axis)
    return lax.ppermute(value, axis, [(source, source + steps) for source in range(count - steps)])


def exchange(value):
    return lax.all_to_all(value, "head", split_axis=0, concat_axis=0, tiled=True)


def after(value, earlier):
    return lax.optimization_barrier((value, earlier))[0]


def pack_kernel(pieces, group, groups, rate_ref, *refs):
    sources = refs[: len(pieces)]
    out_ref, held, came, went = refs[len(pieces) : len(pieces) + 4]
    peers, _, size = out_ref.shape
    rows = held.shape[1]
    inward, outward = [], []
    for d in range(peers):
        at = 0
        for ref, g in zip(sources, pieces):
            for h in range(group):
                n = len(inward)
                column = ((d * groups + g) * group + h) * size
                source = ref.at[:, pl.ds(column, size)]
                inward.append(pltpu.make_async_copy(source, held.at[n], came.at[n]))
                target = out_ref.at[d, pl.ds(at, rows)]
                outward.append(pltpu.make_async_copy(held.at[n], target, went.at[n]))
                at += rows
    for copy in inward:
        copy.start()
    extra = []
    if rate_ref is not None:
        turned, sent = refs[len(pieces) + 4 :]
        heads = rate_ref.shape[0] // peers
        shape = (peers * SUBLANES, rate_ref.shape[0])
        slot = lax.broadcasted_iota(jnp.int32, shape, 0)
        source = lax.broadcasted_iota(jnp.int32, shape, 1)
        chosen = dot(
            (source == slot // SUBLANES * heads + slot % SUBLANES).astype(jnp.bfloat16),
            rate_ref[...],
        )
        turned[:, :, :rows] = chosen.astype(jnp.bfloat16).reshape(peers, SUBLANES, rows)
        for d in range(peers):
            target = out_ref.at[d, pl.ds(at, SUBLANES)]
            extra.append(pltpu.make_async_copy(turned.at[d], target, sent.at[d]))
            extra[-1].start()
    for before, behind in zip(inward, outward):
        before.wait()
        behind.start()
    for copy in outward + extra:
        copy.wait()


def pack(parts, peers, group, groups, size, rates=None):
    rows = parts[0][0].shape[0]
    operands = [array for array, _ in parts]
    pieces = [g for _, g in parts]
    copies = peers * len(parts) * group
    count = len(parts) * group * rows
    specs = [pl.BlockSpec(memory_space=pl.ANY) for _ in parts]
    scratch = [
        pltpu.VMEM((copies, rows, size), jnp.bfloat16),
        pltpu.SemaphoreType.DMA((copies,)),
        pltpu.SemaphoreType.DMA((copies,)),
    ]
    body = functools.partial(pack_kernel, pieces, group, groups)
    if rates is None:
        body = functools.partial(body, None)
    else:
        operands.insert(0, rates)
        specs.insert(0, pl.BlockSpec(memory_space=pltpu.VMEM))
        count += SUBLANES
        scratch += [
            pltpu.VMEM((peers, SUBLANES, size), jnp.bfloat16),
            pltpu.SemaphoreType.DMA((peers,)),
        ]
    return pl.pallas_call(
        body,
        in_specs=specs,
        out_specs=pl.BlockSpec(memory_space=pl.ANY),
        out_shape=jax.ShapeDtypeStruct((peers, count, size), jnp.bfloat16),
        scratch_shapes=scratch,
        compiler_params=PARAMS,
        cost_estimate=cost(0, 4 * peers * count * size),
    )(*operands)


def update_kernel(first_head, k_ref, v_ref, rate_ref, init_ref, out_ref):
    peers, rows, size = k_ref.shape
    head = first_head + pl.program_id(0)
    w_gate, w_up, w_down = init_ref[0, 0], init_ref[1, 0], init_ref[2, 0]
    span = max(1, 512 // rows)
    total = [0.0, 0.0, 0.0]
    for start in range(0, peers, span):
        here = slice(start, start + span)
        tokens = span * rows
        keys = k_ref[here].reshape(tokens, size)
        targets = []
        for s in range(start, start + span):
            turned = jnp.transpose(rate_ref[s].astype(jnp.float32))[:rows]
            lane = lax.broadcasted_iota(jnp.int32, turned.shape, 1)
            rate = jnp.sum(jnp.where(lane == head, turned, 0.0), axis=1, keepdims=True)
            targets.append((rate * v_ref[s].astype(jnp.float32)).astype(jnp.bfloat16))
        targets = jnp.concatenate(targets, axis=0)
        gate_pre = dot_nt(w_gate, keys)
        up_pre = dot_nt(w_up, keys)
        back = dot_nt(w_down, targets)
        sigma = jax.nn.sigmoid(gate_pre)
        gate_act = gate_pre * sigma
        hidden = (gate_act * up_pre).astype(jnp.bfloat16)
        back_gate = (back * up_pre * sigma * (1.0 + gate_pre * (1.0 - sigma))).astype(jnp.bfloat16)
        back_up = (back * gate_act).astype(jnp.bfloat16)
        total[0] += dot(back_gate, keys)
        total[1] += dot(back_up, keys)
        total[2] += dot(hidden, targets)
    for i in range(3):
        out_ref[i, 0] = total[i]


def updates(packed, k_at, v_at, rate_from, fast_init, first_head, group, rows):
    peers, depth, size = rate_from.shape
    hid = fast_init.shape[2]
    length = peers * rows
    block = (peers, rows, size)
    last = depth // SUBLANES - 1
    return pl.pallas_call(
        functools.partial(update_kernel, first_head),
        grid=(group,),
        in_specs=[
            pl.BlockSpec(block, lambda h: (0, k_at + h, 0)),
            pl.BlockSpec(block, lambda h: (0, v_at + h, 0)),
            pl.BlockSpec((peers, SUBLANES, size), lambda h: (0, last, 0)),
            pl.BlockSpec((3, 1, hid, size), lambda h: (0, first_head + h, 0, 0)),
        ],
        out_specs=pl.BlockSpec((3, 1, hid, size), lambda h: (0, h, 0, 0)),
        out_shape=jax.ShapeDtypeStruct((3, group, hid, size), jnp.float32),
        compiler_params=PARAMS,
        cost_estimate=cost(
            group * 6 * 2 * length * size * hid, group * 4 * length * size, group * length * hid
        ),
    )(packed, packed, rate_from, fast_init)


def attend_kernel(place_ref, q_ref, k_ref, v_ref, ek_ref, ev_ref, fit_ref, out_ref):
    peers, rows, size = q_ref.shape
    length = peers * rows
    first = place_ref[0] == 0
    factor = size**-0.5 * LOG2E
    tile = min(256, length)
    span = tile // rows
    flat = lambda ref, low, high: ref[low // rows : high // rows].reshape(high - low, size)
    row = lax.broadcasted_iota(jnp.int32, (tile, tile), 0)
    col = lax.broadcasted_iota(jnp.int32, (tile, tile), 1)
    f_gate, f_up, f_down = fit_ref[0, 0], fit_ref[1, 0], fit_ref[2, 0]
    for start in range(0, length, tile):
        stop = start + tile
        query = flat(q_ref, start, stop)
        far = dot_nt(query, flat(ek_ref, start, length))
        near = dot_nt(query, flat(k_ref, 0, stop))
        far_edge = jnp.where(col > row, far[:, :tile], -jnp.inf)
        near_edge = jnp.where(col <= row, near[:, start:], -jnp.inf)
        far_parts = [far_edge] + ([far[:, tile:]] if far.shape[1] > tile else [])
        near_parts = ([near[:, :start]] if start else []) + [near_edge]
        far = jnp.concatenate(far_parts, axis=1)
        near = jnp.concatenate(near_parts, axis=1)
        top_far = jnp.max(far, axis=1, keepdims=True)
        top_near = jnp.max(near, axis=1, keepdims=True)
        top = jnp.where(first, top_near, jnp.maximum(top_near, top_far))
        shift = top * factor
        shift_far = jnp.where(first, jnp.inf, shift)
        w_far = jnp.exp2(far * factor - shift_far)
        w_near = jnp.exp2(near * factor - shift)
        weight = jnp.sum(w_far, axis=1, keepdims=True) + jnp.sum(w_near, axis=1, keepdims=True)
        attended = dot(w_far.astype(jnp.bfloat16), flat(ev_ref, start, length))
        attended += dot(w_near.astype(jnp.bfloat16), flat(v_ref, 0, stop))
        q_gate = dot_nt(query, f_gate)
        q_up = dot_nt(query, f_up)
        q_hidden = (q_gate * jax.nn.sigmoid(q_gate) * q_up).astype(jnp.bfloat16)
        combined = attended / weight + dot(q_hidden, f_down)
        out_ref[start // rows : stop // rows, 0] = combined.astype(jnp.bfloat16).reshape(
            span, rows, size
        )


def attend(place, q_from, q_at, kv_from, k_at, v_at, edge, ek_at, ev_at, fitted, group, rows):
    peers, _, size = q_from.shape
    hid = fitted.shape[2]
    length = peers * rows
    at = lambda start: pl.BlockSpec((peers, rows, size), lambda h: (0, start + h, 0))
    return pl.pallas_call(
        attend_kernel,
        grid=(group,),
        in_specs=[
            pl.BlockSpec(memory_space=pltpu.SMEM),
            at(q_at),
            at(k_at),
            at(v_at),
            at(ek_at),
            at(ev_at),
            pl.BlockSpec((3, 1, hid, size), lambda h: (0, h, 0, 0)),
        ],
        out_specs=pl.BlockSpec((peers, 1, rows, size), lambda h: (0, h, 0, 0)),
        out_shape=jax.ShapeDtypeStruct((peers, group, rows, size), jnp.bfloat16),
        compiler_params=PARAMS,
        cost_estimate=cost(
            group * length * size * 2 * (2 * (WINDOW + 256) + 3 * hid),
            group * 12 * length * size,
            group * length * (WINDOW + 256),
        ),
    )(place, q_from, kv_from, kv_from, edge, edge, fitted)


def norm_kernel(*refs):
    *sources, gain_ref, out_ref = refs
    peers, group, rows, size = sources[0].shape
    heads = group * len(sources)
    width = out_ref.shape[1]
    square = jnp.zeros((rows, size), jnp.float32)
    for ref in sources:
        for s in range(peers):
            for h in range(group):
                x = ref[s, h].astype(jnp.float32)
                square += x * x
    factor = lax.rsqrt(jnp.sum(square, axis=1, keepdims=True) / width + EPSILON)
    for number, ref in enumerate(sources):
        for s in range(peers):
            for h in range(group):
                low = (s * heads + number * group + h) * size
                x = ref[s, h].astype(jnp.float32)
                out_ref[:, low : low + size] = (
                    x * factor * gain_ref[:, low : low + size]
                ).astype(jnp.bfloat16)


def normalize(parts, gain):
    peers, group, rows, size = parts[0].shape
    width = gain.shape[0]
    step = min(128, rows)
    return pl.pallas_call(
        norm_kernel,
        grid=(rows // step,),
        in_specs=[pl.BlockSpec((peers, group, step, size), lambda i: (0, 0, i, 0)) for _ in parts]
        + [pl.BlockSpec((1, width), lambda i: (0, 0))],
        out_specs=pl.BlockSpec((step, width), lambda i: (i, 0)),
        out_shape=jax.ShapeDtypeStruct((rows, width), jnp.bfloat16),
        compiler_params=PARAMS,
        cost_estimate=cost(5 * rows * width, 4 * rows * width),
    )(*parts, gain.reshape(1, width))


def earlier_sum(value, axis):
    before = jnp.zeros_like(value)
    for step in range(1, lax.axis_size(axis)):
        running = (value + before).astype(jnp.bfloat16)
        before = before + lax.ppermute(running, axis, [(step - 1, step)]).astype(jnp.float32)
    return before


def refit(initial, before):
    initial = initial.astype(jnp.float32)
    target_ms = jnp.mean(initial * initial, axis=3, keepdims=True)
    renewed = initial + before
    current = jnp.mean(renewed * renewed, axis=3, keepdims=True)
    return (renewed * jnp.sqrt(target_ms) * lax.rsqrt(current + EPSILON)).astype(jnp.bfloat16)


def on_device(queries, keys, values, rates, fast_init, gain):
    peers = lax.axis_size("head")
    rows = queries.shape[0]
    heads = fast_init.shape[1]
    size = fast_init.shape[3]
    groups = 2
    group = heads // groups
    place = lax.axis_index("ctx").astype(jnp.int32).reshape(1)
    lay = lambda *parts, **more: pack(parts, peers, group, groups, size, **more)

    kv_a = exchange(lay((keys, 0), (values, 0), rates=rates.T))
    kv_a, kvq = lax.optimization_barrier((kv_a, lay((keys, 1), (values, 1), (queries, 0))))
    kvq = exchange(kvq)
    edge_a = from_behind(kv_a, "ctx", 1)
    up_a = updates(kv_a, 0, group, kv_a, fast_init, 0, group, rows)
    fit_a = refit(fast_init[:, :group], earlier_sum(up_a, "ctx"))
    kvq, q_b, fit_a = lax.optimization_barrier((kvq, lay((queries, 1)), fit_a))
    q_b = exchange(q_b)
    kv_b = kvq[:, : 2 * group * rows]
    edge_b = from_behind(kv_b, "ctx", 1)
    up_b = updates(kv_b, 0, group, kv_a, fast_init, group, group, rows)
    fit_b = refit(fast_init[:, group:], earlier_sum(up_b, "ctx"))
    fit_a = after(fit_a, up_b)
    out_a = attend(place, kvq, 2 * group, kv_a, 0, group, edge_a, 0, group, fit_a, group, rows)
    back_a = exchange(after(out_a, q_b))
    out_b = attend(place, q_b, 0, kv_b, 0, group, edge_b, 0, group, fit_b, group, rows)
    back_b = exchange(after(out_b, back_a))
    return normalize([back_a, back_b], gain)


def solution(mesh):
    rows = P(("ctx", "head"), None)
    in_specs = (rows, rows, rows, rows, P(None, "head", None, None), P())
    return jax.shard_map(on_device, mesh=mesh, in_specs=in_specs, out_specs=rows, check_vma=False)
```

```python
import functools

import jax
import jax.numpy as jnp
from jax import lax
from jax.experimental import pallas as pl
from jax.experimental.pallas import tpu as pltpu
from jax.sharding import PartitionSpec as P

WINDOW = 2048
EPSILON = 1e-06
LOG2E = 1.4426950408889634
NT = (((1,), (1,)), ((), ()))
SUBLANES = 16
PARAMS = pltpu.CompilerParams(vmem_limit_bytes=60 << 20)
COST = 0.001


def dot(a, b):
    return jnp.dot(a, b, preferred_element_type=jnp.float32)


def dot_nt(a, b):
    return lax.dot_general(a, b, NT, preferred_element_type=jnp.float32)


def cost(flops, bytes_accessed, transcendentals=0):
    return pl.CostEstimate(
        flops=int(flops * COST),
        bytes_accessed=int(bytes_accessed * COST),
        transcendentals=int(transcendentals * COST),
    )


def from_behind(value, axis, steps):
    count = lax.axis_size(axis)
    return lax.ppermute(value, axis, [(source, source + steps) for source in range(count - steps)])


def exchange(value):
    return lax.all_to_all(value, "head", split_axis=0, concat_axis=0, tiled=True)


def after(value, earlier):
    return lax.optimization_barrier((value, earlier))[0]


def pack_kernel(pieces, group, groups, rate_ref, *refs):
    sources = refs[: len(pieces)]
    out_ref, held, came, went = refs[len(pieces) : len(pieces) + 4]
    peers, _, size = out_ref.shape
    rows = held.shape[1]
    inward, outward = [], []
    for d in range(peers):
        at = 0
        for ref, g in zip(sources, pieces):
            for h in range(group):
                n = len(inward)
                column = ((d * groups + g) * group + h) * size
                source = ref.at[:, pl.ds(column, size)]
                inward.append(pltpu.make_async_copy(source, held.at[n], came.at[n]))
                target = out_ref.at[d, pl.ds(at, rows)]
                outward.append(pltpu.make_async_copy(held.at[n], target, went.at[n]))
                at += rows
    for copy in inward:
        copy.start()
    extra = []
    if rate_ref is not None:
        turned, sent = refs[len(pieces) + 4 :]
        heads = rate_ref.shape[0] // peers
        shape = (peers * SUBLANES, rate_ref.shape[0])
        slot = lax.broadcasted_iota(jnp.int32, shape, 0)
        source = lax.broadcasted_iota(jnp.int32, shape, 1)
        chosen = dot(
            (source == slot // SUBLANES * heads + slot % SUBLANES).astype(jnp.bfloat16),
            rate_ref[...],
        )
        turned[:, :, :rows] = chosen.astype(jnp.bfloat16).reshape(peers, SUBLANES, rows)
        for d in range(peers):
            target = out_ref.at[d, pl.ds(at, SUBLANES)]
            extra.append(pltpu.make_async_copy(turned.at[d], target, sent.at[d]))
            extra[-1].start()
    for before, behind in zip(inward, outward):
        before.wait()
        behind.start()
    for copy in outward + extra:
        copy.wait()


def pack(parts, peers, group, groups, size, rates=None):
    rows = parts[0][0].shape[0]
    operands = [array for array, _ in parts]
    pieces = [g for _, g in parts]
    copies = peers * len(parts) * group
    count = len(parts) * group * rows
    specs = [pl.BlockSpec(memory_space=pl.ANY) for _ in parts]
    scratch = [
        pltpu.VMEM((copies, rows, size), jnp.bfloat16),
        pltpu.SemaphoreType.DMA((copies,)),
        pltpu.SemaphoreType.DMA((copies,)),
    ]
    body = functools.partial(pack_kernel, pieces, group, groups)
    if rates is None:
        body = functools.partial(body, None)
    else:
        operands.insert(0, rates)
        specs.insert(0, pl.BlockSpec(memory_space=pltpu.VMEM))
        count += SUBLANES
        scratch += [
            pltpu.VMEM((peers, SUBLANES, size), jnp.bfloat16),
            pltpu.SemaphoreType.DMA((peers,)),
        ]
    return pl.pallas_call(
        body,
        in_specs=specs,
        out_specs=pl.BlockSpec(memory_space=pl.ANY),
        out_shape=jax.ShapeDtypeStruct((peers, count, size), jnp.bfloat16),
        scratch_shapes=scratch,
        compiler_params=PARAMS,
        cost_estimate=cost(0, 4 * peers * count * size),
    )(*operands)


def update_kernel(first_head, k_ref, v_ref, rate_ref, init_ref, out_ref):
    peers, rows, size = k_ref.shape
    head = first_head + pl.program_id(0)
    w_gate, w_up, w_down = init_ref[0, 0], init_ref[1, 0], init_ref[2, 0]
    span = max(1, 512 // rows)
    total = [0.0, 0.0, 0.0]
    for start in range(0, peers, span):
        here = slice(start, start + span)
        tokens = span * rows
        keys = k_ref[here].reshape(tokens, size)
        targets = []
        for s in range(start, start + span):
            turned = jnp.transpose(rate_ref[s].astype(jnp.float32))[:rows]
            lane = lax.broadcasted_iota(jnp.int32, turned.shape, 1)
            rate = jnp.sum(jnp.where(lane == head, turned, 0.0), axis=1, keepdims=True)
            targets.append((rate * v_ref[s].astype(jnp.float32)).astype(jnp.bfloat16))
        targets = jnp.concatenate(targets, axis=0)
        gate_pre = dot_nt(w_gate, keys)
        up_pre = dot_nt(w_up, keys)
        back = dot_nt(w_down, targets)
        sigma = jax.nn.sigmoid(gate_pre)
        gate_act = gate_pre * sigma
        hidden = (gate_act * up_pre).astype(jnp.bfloat16)
        back_gate = (back * up_pre * sigma * (1.0 + gate_pre * (1.0 - sigma))).astype(jnp.bfloat16)
        back_up = (back * gate_act).astype(jnp.bfloat16)
        total[0] += dot(back_gate, keys)
        total[1] += dot(back_up, keys)
        total[2] += dot(hidden, targets)
    for i in range(3):
        out_ref[i, 0] = total[i]


def updates(packed, k_at, v_at, rate_from, fast_init, first_head, group, rows):
    peers, depth, size = rate_from.shape
    hid = fast_init.shape[2]
    length = peers * rows
    block = (peers, rows, size)
    last = depth // SUBLANES - 1
    return pl.pallas_call(
        functools.partial(update_kernel, first_head),
        grid=(group,),
        in_specs=[
            pl.BlockSpec(block, lambda h: (0, k_at + h, 0)),
            pl.BlockSpec(block, lambda h: (0, v_at + h, 0)),
            pl.BlockSpec((peers, SUBLANES, size), lambda h: (0, last, 0)),
            pl.BlockSpec((3, 1, hid, size), lambda h: (0, first_head + h, 0, 0)),
        ],
        out_specs=pl.BlockSpec((3, 1, hid, size), lambda h: (0, h, 0, 0)),
        out_shape=jax.ShapeDtypeStruct((3, group, hid, size), jnp.float32),
        compiler_params=PARAMS,
        cost_estimate=cost(
            group * 6 * 2 * length * size * hid, group * 4 * length * size, group * length * hid
        ),
    )(packed, packed, rate_from, fast_init)


def attend_kernel(place_ref, q_ref, k_ref, v_ref, ek_ref, ev_ref, fit_ref, *refs):
    peers, rows, size = q_ref.shape
    length = peers * rows
    first = place_ref[0] == 0
    factor = size**-0.5 * LOG2E
    tile = min(256, length)
    span = tile // rows
    flat = lambda ref, low, high: ref[low // rows : high // rows].reshape(high - low, size)
    row = lax.broadcasted_iota(jnp.int32, (tile, tile), 0)
    col = lax.broadcasted_iota(jnp.int32, (tile, tile), 1)
    f_gate, f_up, f_down = fit_ref[0, 0], fit_ref[1, 0], fit_ref[2, 0]
    for start in range(0, length, tile):
        stop = start + tile
        query = flat(q_ref, start, stop)
        far = dot_nt(query, flat(ek_ref, start, length))
        near = dot_nt(query, flat(k_ref, 0, stop))
        far_edge = jnp.where(col > row, far[:, :tile], -jnp.inf)
        near_edge = jnp.where(col <= row, near[:, start:], -jnp.inf)
        far_parts = [far_edge] + ([far[:, tile:]] if far.shape[1] > tile else [])
        near_parts = ([near[:, :start]] if start else []) + [near_edge]
        far = jnp.concatenate(far_parts, axis=1)
        near = jnp.concatenate(near_parts, axis=1)
        top_far = jnp.max(far, axis=1, keepdims=True)
        top_near = jnp.max(near, axis=1, keepdims=True)
        top = jnp.where(first, top_near, jnp.maximum(top_near, top_far))
        shift = top * factor
        shift_far = jnp.where(first, jnp.inf, shift)
        w_far = jnp.exp2(far * factor - shift_far)
        w_near = jnp.exp2(near * factor - shift)
        weight = jnp.sum(w_far, axis=1, keepdims=True) + jnp.sum(w_near, axis=1, keepdims=True)
        attended = dot(w_far.astype(jnp.bfloat16), flat(ev_ref, start, length))
        attended += dot(w_near.astype(jnp.bfloat16), flat(v_ref, 0, stop))
        q_gate = dot_nt(query, f_gate)
        q_up = dot_nt(query, f_up)
        q_hidden = (q_gate * jax.nn.sigmoid(q_gate) * q_up).astype(jnp.bfloat16)
        combined = attended / weight + dot(q_hidden, f_down)
        combined = combined.astype(jnp.bfloat16).reshape(span, rows, size)
        if len(refs) == 1:
            refs[0][start // rows : stop // rows, 0] = combined
        else:
            for n in range(span):
                refs[-1][place_ref[1] ^ (start // rows + n)] = combined[n]
    for step, out_ref in enumerate(refs[:-1]):
        out_ref[0] = refs[-1][step]


def attend(place, q_from, q_at, kv_from, k_at, v_at, edge, ek_at, ev_at, fitted, group, rows, split):
    peers, _, size = q_from.shape
    hid = fitted.shape[2]
    length = peers * rows
    at = lambda start: pl.BlockSpec((peers, rows, size), lambda h: (0, start + h, 0))
    return pl.pallas_call(
        attend_kernel,
        grid=(group,),
        in_specs=[
            pl.BlockSpec(memory_space=pltpu.SMEM),
            at(q_at),
            at(k_at),
            at(v_at),
            at(ek_at),
            at(ev_at),
            pl.BlockSpec((3, 1, hid, size), lambda h: (0, h, 0, 0)),
        ],
        out_specs=[pl.BlockSpec((1, rows, size), lambda h: (h, 0, 0))] * peers
        if split
        else pl.BlockSpec((peers, 1, rows, size), lambda h: (0, h, 0, 0)),
        out_shape=[jax.ShapeDtypeStruct((group, rows, size), jnp.bfloat16)] * peers
        if split
        else jax.ShapeDtypeStruct((peers, group, rows, size), jnp.bfloat16),
        scratch_shapes=[pltpu.VMEM((peers, rows, size), jnp.bfloat16)] if split else [],
        compiler_params=PARAMS,
        cost_estimate=cost(
            group * length * size * 2 * (2 * (WINDOW + 256) + 3 * hid),
            group * 12 * length * size,
            group * length * (WINDOW + 256),
        ),
    )(place, q_from, kv_from, kv_from, edge, edge, fitted)


def swap_order(count):
    short = [step for step in (1, 2) if step < count]
    return short + list(range(count - 1, 2, -1)) + [0]


def swap(pieces):
    count = lax.axis_size("head")
    return [
        lax.ppermute(pieces[step], "head", [(i, i ^ step) for i in range(count)])
        if step
        else pieces[0]
        for step in swap_order(count)
    ]


def norm_kernel(place_ref, first_ref, *refs):
    *pieces, gain_ref, out_ref = refs
    peers, group, rows, size = first_ref.shape
    width = out_ref.shape[1]
    parts = [(lambda p=p, h=h: first_ref[p, h], p * 2 * group + h) for p in range(peers) for h in range(group)]
    for step, ref in zip(swap_order(peers), pieces):
        p = place_ref[1] ^ step
        parts += [(lambda ref=ref, h=h: ref[h], (p * 2 + 1) * group + h) for h in range(group)]
    square = jnp.zeros((rows, size), jnp.float32)
    for load, _ in parts:
        x = load().astype(jnp.float32)
        square += x * x
    factor = lax.rsqrt(jnp.sum(square, axis=1, keepdims=True) / width + EPSILON)
    for load, head in parts:
        here = pl.ds(pl.multiple_of(head * size, size), size)
        x = load().astype(jnp.float32)
        out_ref[:, here] = (x * factor * gain_ref[:, here]).astype(jnp.bfloat16)


def normalize(place, first, pieces, gain):
    peers, group, rows, size = first.shape
    width = gain.shape[0]
    step = min(128, rows)
    return pl.pallas_call(
        norm_kernel,
        grid=(rows // step,),
        in_specs=[
            pl.BlockSpec(memory_space=pltpu.SMEM),
            pl.BlockSpec((peers, group, step, size), lambda i: (0, 0, i, 0)),
        ]
        + [pl.BlockSpec((group, step, size), lambda i: (0, i, 0)) for _ in pieces]
        + [pl.BlockSpec((1, width), lambda i: (0, 0))],
        out_specs=pl.BlockSpec((step, width), lambda i: (i, 0)),
        out_shape=jax.ShapeDtypeStruct((rows, width), jnp.bfloat16),
        compiler_params=PARAMS,
        cost_estimate=cost(5 * rows * width, 4 * rows * width),
    )(place, first, *pieces, gain.reshape(1, width))


def earlier_sum(value, axis, dtype):
    before = jnp.zeros_like(value)
    for step in range(1, lax.axis_size(axis)):
        running = (value + before).astype(dtype)
        before = before + lax.ppermute(running, axis, [(step - 1, step)]).astype(jnp.float32)
    return before


def refit(initial, before):
    initial = initial.astype(jnp.float32)
    target_ms = jnp.mean(initial * initial, axis=3, keepdims=True)
    renewed = initial + before
    current = jnp.mean(renewed * renewed, axis=3, keepdims=True)
    return (renewed * jnp.sqrt(target_ms) * lax.rsqrt(current + EPSILON)).astype(jnp.bfloat16)


def on_device(queries, keys, values, rates, fast_init, gain):
    peers = lax.axis_size("head")
    rows = queries.shape[0]
    heads = fast_init.shape[1]
    size = fast_init.shape[3]
    groups = 2
    group = heads // groups
    place = jnp.stack([lax.axis_index("ctx"), lax.axis_index("head")]).astype(jnp.int32)
    lay = lambda *parts, **more: pack(parts, peers, group, groups, size, **more)

    kv_a = exchange(lay((keys, 0), (values, 0), rates=rates.T))
    kv_a, kvq = lax.optimization_barrier((kv_a, lay((keys, 1), (values, 1), (queries, 0))))
    kvq = exchange(kvq)
    edge_a = from_behind(kv_a, "ctx", 1)
    up_a = updates(kv_a, 0, group, kv_a, fast_init, 0, group, rows)
    fit_a = refit(fast_init[:, :group], earlier_sum(up_a, "ctx", jnp.float32))
    kvq, q_b, fit_a = lax.optimization_barrier((kvq, lay((queries, 1)), fit_a))
    q_b = exchange(q_b)
    kv_b = kvq[:, : 2 * group * rows]
    edge_b = from_behind(kv_b, "ctx", 1)
    up_b = updates(kv_b, 0, group, kv_a, fast_init, group, group, rows)
    fit_b = refit(fast_init[:, group:], earlier_sum(up_b, "ctx", jnp.bfloat16))
    fit_a = after(fit_a, up_b)
    out_a = attend(place, kvq, 2 * group, kv_a, 0, group, edge_a, 0, group, fit_a, group, rows, False)
    back_a = exchange(after(out_a, q_b))
    out_b = attend(place, q_b, 0, kv_b, 0, group, edge_b, 0, group, fit_b, group, rows, True)
    return normalize(place, back_a, swap(out_b), gain)


def solution(mesh):
    rows = P(("ctx", "head"), None)
    in_specs = (rows, rows, rows, rows, P(None, "head", None, None), P())
    return jax.shard_map(on_device, mesh=mesh, in_specs=in_specs, out_specs=rows, check_vma=False)
```

```python
import functools

import jax
import jax.numpy as jnp
from jax import lax
from jax.experimental import pallas as pl
from jax.experimental.pallas import tpu as pltpu
from jax.sharding import PartitionSpec as P

WINDOW = 2048
EPSILON = 1e-06
LOG2E = 1.4426950408889634
NT = (((1,), (1,)), ((), ()))
SUBLANES = 16
PARAMS = pltpu.CompilerParams(vmem_limit_bytes=60 << 20)
COST = 0.001


def dot(a, b):
    return jnp.dot(a, b, preferred_element_type=jnp.float32)


def dot_nt(a, b):
    return lax.dot_general(a, b, NT, preferred_element_type=jnp.float32)


def cost(flops, bytes_accessed, transcendentals=0):
    return pl.CostEstimate(
        flops=int(flops * COST),
        bytes_accessed=int(bytes_accessed * COST),
        transcendentals=int(transcendentals * COST),
    )


def from_behind(value, axis, steps):
    count = lax.axis_size(axis)
    return lax.ppermute(value, axis, [(source, source + steps) for source in range(count - steps)])


def exchange(value):
    return lax.all_to_all(value, "head", split_axis=0, concat_axis=0, tiled=True)


def after(value, earlier):
    return lax.optimization_barrier((value, earlier))[0]


def pack_kernel(pieces, group, groups, rate_ref, *refs):
    sources = refs[: len(pieces)]
    out_ref, held, came, went = refs[len(pieces) : len(pieces) + 4]
    peers, _, size = out_ref.shape
    rows = held.shape[1]
    inward, outward = [], []
    for d in range(peers):
        at = 0
        for ref, g in zip(sources, pieces):
            for h in range(group):
                n = len(inward)
                column = ((d * groups + g) * group + h) * size
                source = ref.at[:, pl.ds(column, size)]
                inward.append(pltpu.make_async_copy(source, held.at[n], came.at[n]))
                target = out_ref.at[d, pl.ds(at, rows)]
                outward.append(pltpu.make_async_copy(held.at[n], target, went.at[n]))
                at += rows
    for copy in inward:
        copy.start()
    extra = []
    if rate_ref is not None:
        turned, sent = refs[len(pieces) + 4 :]
        heads = rate_ref.shape[0] // peers
        shape = (peers * SUBLANES, rate_ref.shape[0])
        slot = lax.broadcasted_iota(jnp.int32, shape, 0)
        source = lax.broadcasted_iota(jnp.int32, shape, 1)
        chosen = dot(
            (source == slot // SUBLANES * heads + slot % SUBLANES).astype(jnp.bfloat16),
            rate_ref[...],
        )
        turned[:, :, :rows] = chosen.astype(jnp.bfloat16).reshape(peers, SUBLANES, rows)
        for d in range(peers):
            target = out_ref.at[d, pl.ds(at, SUBLANES)]
            extra.append(pltpu.make_async_copy(turned.at[d], target, sent.at[d]))
            extra[-1].start()
    for before, behind in zip(inward, outward):
        before.wait()
        behind.start()
    for copy in outward + extra:
        copy.wait()


def pack(parts, peers, group, groups, size, rates=None):
    rows = parts[0][0].shape[0]
    operands = [array for array, _ in parts]
    pieces = [g for _, g in parts]
    copies = peers * len(parts) * group
    count = len(parts) * group * rows
    specs = [pl.BlockSpec(memory_space=pl.ANY) for _ in parts]
    scratch = [
        pltpu.VMEM((copies, rows, size), jnp.bfloat16),
        pltpu.SemaphoreType.DMA((copies,)),
        pltpu.SemaphoreType.DMA((copies,)),
    ]
    body = functools.partial(pack_kernel, pieces, group, groups)
    if rates is None:
        body = functools.partial(body, None)
    else:
        operands.insert(0, rates)
        specs.insert(0, pl.BlockSpec(memory_space=pltpu.VMEM))
        count += SUBLANES
        scratch += [
            pltpu.VMEM((peers, SUBLANES, size), jnp.bfloat16),
            pltpu.SemaphoreType.DMA((peers,)),
        ]
    return pl.pallas_call(
        body,
        in_specs=specs,
        out_specs=pl.BlockSpec(memory_space=pl.ANY),
        out_shape=jax.ShapeDtypeStruct((peers, count, size), jnp.bfloat16),
        scratch_shapes=scratch,
        compiler_params=PARAMS,
        cost_estimate=cost(0, 4 * peers * count * size),
    )(*operands)


def update_kernel(first_head, k_ref, v_ref, rate_ref, init_ref, out_ref):
    peers, rows, size = k_ref.shape
    head = first_head + pl.program_id(0)
    w_gate, w_up, w_down = init_ref[0, 0], init_ref[1, 0], init_ref[2, 0]
    span = max(1, 512 // rows)
    total = [0.0, 0.0, 0.0]
    for start in range(0, peers, span):
        here = slice(start, start + span)
        tokens = span * rows
        keys = k_ref[here].reshape(tokens, size)
        targets = []
        for s in range(start, start + span):
            turned = jnp.transpose(rate_ref[s].astype(jnp.float32))[:rows]
            lane = lax.broadcasted_iota(jnp.int32, turned.shape, 1)
            rate = jnp.sum(jnp.where(lane == head, turned, 0.0), axis=1, keepdims=True)
            targets.append((rate * v_ref[s].astype(jnp.float32)).astype(jnp.bfloat16))
        targets = jnp.concatenate(targets, axis=0)
        gate_pre = dot_nt(w_gate, keys)
        up_pre = dot_nt(w_up, keys)
        back = dot_nt(w_down, targets)
        sigma = jax.nn.sigmoid(gate_pre)
        gate_act = gate_pre * sigma
        hidden = (gate_act * up_pre).astype(jnp.bfloat16)
        back_gate = (back * up_pre * sigma * (1.0 + gate_pre * (1.0 - sigma))).astype(jnp.bfloat16)
        back_up = (back * gate_act).astype(jnp.bfloat16)
        total[0] += dot(back_gate, keys)
        total[1] += dot(back_up, keys)
        total[2] += dot(hidden, targets)
    for i in range(3):
        out_ref[i, 0] = total[i]


def updates(packed, k_at, v_at, rate_from, fast_init, first_head, group, rows):
    peers, depth, size = rate_from.shape
    hid = fast_init.shape[2]
    length = peers * rows
    block = (peers, rows, size)
    last = depth // SUBLANES - 1
    return pl.pallas_call(
        functools.partial(update_kernel, first_head),
        grid=(group,),
        in_specs=[
            pl.BlockSpec(block, lambda h: (0, k_at + h, 0)),
            pl.BlockSpec(block, lambda h: (0, v_at + h, 0)),
            pl.BlockSpec((peers, SUBLANES, size), lambda h: (0, last, 0)),
            pl.BlockSpec((3, 1, hid, size), lambda h: (0, first_head + h, 0, 0)),
        ],
        out_specs=pl.BlockSpec((3, 1, hid, size), lambda h: (0, h, 0, 0)),
        out_shape=jax.ShapeDtypeStruct((3, group, hid, size), jnp.float32),
        compiler_params=PARAMS,
        cost_estimate=cost(
            group * 6 * 2 * length * size * hid, group * 4 * length * size, group * length * hid
        ),
    )(packed, packed, rate_from, fast_init)


def attend_kernel(place_ref, q_ref, k_ref, v_ref, ek_ref, ev_ref, fit_ref, *refs):
    peers, rows, size = q_ref.shape
    length = peers * rows
    first = place_ref[0] == 0
    factor = size**-0.5 * LOG2E
    tile = min(256, length)
    span = tile // rows
    flat = lambda ref, low, high: ref[low // rows : high // rows].reshape(high - low, size)
    row = lax.broadcasted_iota(jnp.int32, (tile, tile), 0)
    col = lax.broadcasted_iota(jnp.int32, (tile, tile), 1)
    f_gate, f_up, f_down = fit_ref[0, 0], fit_ref[1, 0], fit_ref[2, 0]
    for start in range(0, length, tile):
        stop = start + tile
        query = flat(q_ref, start, stop)
        far = dot_nt(query, flat(ek_ref, start, length))
        near = dot_nt(query, flat(k_ref, 0, stop))
        far_edge = jnp.where(col > row, far[:, :tile], -jnp.inf)
        near_edge = jnp.where(col <= row, near[:, start:], -jnp.inf)
        far_parts = [far_edge] + ([far[:, tile:]] if far.shape[1] > tile else [])
        near_parts = ([near[:, :start]] if start else []) + [near_edge]
        far = jnp.concatenate(far_parts, axis=1)
        near = jnp.concatenate(near_parts, axis=1)
        top_far = jnp.max(far, axis=1, keepdims=True)
        top_near = jnp.max(near, axis=1, keepdims=True)
        top = jnp.where(first, top_near, jnp.maximum(top_near, top_far))
        w_far = jnp.exp2((far - jnp.where(first, jnp.inf, top)) * factor)
        w_near = jnp.exp2((near - top) * factor)
        weight = jnp.sum(w_far, axis=1, keepdims=True) + jnp.sum(w_near, axis=1, keepdims=True)
        attended = dot(w_far.astype(jnp.bfloat16), flat(ev_ref, start, length))
        attended += dot(w_near.astype(jnp.bfloat16), flat(v_ref, 0, stop))
        q_gate = dot_nt(query, f_gate)
        q_up = dot_nt(query, f_up)
        q_hidden = (q_gate * jax.nn.sigmoid(q_gate) * q_up).astype(jnp.bfloat16)
        combined = attended / weight + dot(q_hidden, f_down)
        combined = combined.astype(jnp.bfloat16).reshape(span, rows, size)
        if len(refs) == 1:
            refs[0][start // rows : stop // rows, 0] = combined
        else:
            for n in range(span):
                refs[-1][place_ref[1] ^ (start // rows + n)] = combined[n]
    for step, out_ref in enumerate(refs[:-1]):
        out_ref[0] = refs[-1][step]


def attend(place, q_from, q_at, kv_from, k_at, v_at, edge, ek_at, ev_at, fitted, group, rows, split):
    peers, _, size = q_from.shape
    hid = fitted.shape[2]
    length = peers * rows
    at = lambda start: pl.BlockSpec((peers, rows, size), lambda h: (0, start + h, 0))
    return pl.pallas_call(
        attend_kernel,
        grid=(group,),
        in_specs=[
            pl.BlockSpec(memory_space=pltpu.SMEM),
            at(q_at),
            at(k_at),
            at(v_at),
            at(ek_at),
            at(ev_at),
            pl.BlockSpec((3, 1, hid, size), lambda h: (0, h, 0, 0)),
        ],
        out_specs=[pl.BlockSpec((1, rows, size), lambda h: (h, 0, 0))] * peers
        if split
        else pl.BlockSpec((peers, 1, rows, size), lambda h: (0, h, 0, 0)),
        out_shape=[jax.ShapeDtypeStruct((group, rows, size), jnp.bfloat16)] * peers
        if split
        else jax.ShapeDtypeStruct((peers, group, rows, size), jnp.bfloat16),
        scratch_shapes=[pltpu.VMEM((peers, rows, size), jnp.bfloat16)] if split else [],
        compiler_params=PARAMS,
        cost_estimate=cost(
            group * length * size * 2 * (2 * (WINDOW + 256) + 3 * hid),
            group * 12 * length * size,
            group * length * (WINDOW + 256),
        ),
    )(place, q_from, kv_from, kv_from, edge, edge, fitted)


def swap_order(count):
    short = [step for step in (1, 2) if step < count]
    return short + list(range(count - 1, 2, -1)) + [0]


def swap(pieces):
    count = lax.axis_size("head")
    return [
        lax.ppermute(pieces[step], "head", [(i, i ^ step) for i in range(count)])
        if step
        else pieces[0]
        for step in swap_order(count)
    ]


def norm_kernel(place_ref, first_ref, *refs):
    *pieces, gain_ref, out_ref = refs
    peers, group, rows, size = first_ref.shape
    width = out_ref.shape[1]
    parts = [(lambda p=p, h=h: first_ref[p, h], p * 2 * group + h) for p in range(peers) for h in range(group)]
    for step, ref in zip(swap_order(peers), pieces):
        p = place_ref[1] ^ step
        parts += [(lambda ref=ref, h=h: ref[h], (p * 2 + 1) * group + h) for h in range(group)]
    square = jnp.zeros((rows, size), jnp.float32)
    for load, _ in parts:
        x = load().astype(jnp.float32)
        square += x * x
    factor = lax.rsqrt(jnp.sum(square, axis=1, keepdims=True) / width + EPSILON)
    for load, head in parts:
        here = pl.ds(pl.multiple_of(head * size, size), size)
        x = load().astype(jnp.float32)
        out_ref[:, here] = (x * factor * gain_ref[:, here]).astype(jnp.bfloat16)


def normalize(place, first, pieces, gain):
    peers, group, rows, size = first.shape
    width = gain.shape[0]
    step = min(128, rows)
    return pl.pallas_call(
        norm_kernel,
        grid=(rows // step,),
        in_specs=[
            pl.BlockSpec(memory_space=pltpu.SMEM),
            pl.BlockSpec((peers, group, step, size), lambda i: (0, 0, i, 0)),
        ]
        + [pl.BlockSpec((group, step, size), lambda i: (0, i, 0)) for _ in pieces]
        + [pl.BlockSpec((1, width), lambda i: (0, 0))],
        out_specs=pl.BlockSpec((step, width), lambda i: (i, 0)),
        out_shape=jax.ShapeDtypeStruct((rows, width), jnp.bfloat16),
        compiler_params=PARAMS,
        cost_estimate=cost(5 * rows * width, 4 * rows * width),
    )(place, first, *pieces, gain.reshape(1, width))


def earlier_sum(value, axis, dtype):
    before = jnp.zeros_like(value)
    for step in range(1, lax.axis_size(axis)):
        running = (value + before).astype(dtype)
        before = before + lax.ppermute(running, axis, [(step - 1, step)]).astype(jnp.float32)
    return before


def refit(initial, before):
    initial = initial.astype(jnp.float32)
    target_ms = jnp.mean(initial * initial, axis=3, keepdims=True)
    renewed = initial + before
    current = jnp.mean(renewed * renewed, axis=3, keepdims=True)
    return (renewed * jnp.sqrt(target_ms) * lax.rsqrt(current + EPSILON)).astype(jnp.bfloat16)


def on_device(queries, keys, values, rates, fast_init, gain):
    peers = lax.axis_size("head")
    rows = queries.shape[0]
    heads = fast_init.shape[1]
    size = fast_init.shape[3]
    groups = 2
    group = heads // groups
    place = jnp.stack([lax.axis_index("ctx"), lax.axis_index("head")]).astype(jnp.int32)
    lay = lambda *parts, **more: pack(parts, peers, group, groups, size, **more)

    kv_a = exchange(lay((keys, 0), (values, 0), rates=rates.T))
    kv_a, kvq = lax.optimization_barrier((kv_a, lay((keys, 1), (values, 1), (queries, 0))))
    kvq = exchange(kvq)
    edge_a = from_behind(kv_a, "ctx", 1)
    up_a = updates(kv_a, 0, group, kv_a, fast_init, 0, group, rows)
    fit_a = refit(fast_init[:, :group], earlier_sum(up_a, "ctx", jnp.float32))
    kvq, q_b, fit_a = lax.optimization_barrier((kvq, lay((queries, 1)), fit_a))
    q_b = exchange(q_b)
    kv_b = kvq[:, : 2 * group * rows]
    edge_b = from_behind(kv_b, "ctx", 1)
    up_b = updates(kv_b, 0, group, kv_a, fast_init, group, group, rows)
    fit_b = refit(fast_init[:, group:], earlier_sum(up_b, "ctx", jnp.bfloat16))
    fit_a = after(fit_a, up_b)
    out_a = attend(place, kvq, 2 * group, kv_a, 0, group, edge_a, 0, group, fit_a, group, rows, False)
    back_a = exchange(after(out_a, q_b))
    out_b = attend(place, q_b, 0, kv_b, 0, group, edge_b, 0, group, fit_b, group, rows, True)
    return normalize(place, back_a, swap(out_b), gain)


def solution(mesh):
    rows = P(("ctx", "head"), None)
    in_specs = (rows, rows, rows, rows, P(None, "head", None, None), P())
    return jax.shard_map(on_device, mesh=mesh, in_specs=in_specs, out_specs=rows, check_vma=False)
```

```python
import functools

import jax
import jax.numpy as jnp
from jax import lax
from jax.experimental import pallas as pl
from jax.experimental.pallas import tpu as pltpu
from jax.sharding import PartitionSpec as P

WINDOW = 2048
EPSILON = 1e-06
LOG2E = 1.4426950408889634
NT = (((1,), (1,)), ((), ()))
SUBLANES = 16
PARAMS = pltpu.CompilerParams(vmem_limit_bytes=60 << 20)
COST = 0.001


def dot(a, b):
    return jnp.dot(a, b, preferred_element_type=jnp.float32)


def dot_nt(a, b):
    return lax.dot_general(a, b, NT, preferred_element_type=jnp.float32)


def cost(flops, bytes_accessed, transcendentals=0):
    return pl.CostEstimate(
        flops=int(flops * COST),
        bytes_accessed=int(bytes_accessed * COST),
        transcendentals=int(transcendentals * COST),
    )


def from_behind(value, axis, steps):
    count = lax.axis_size(axis)
    return lax.ppermute(value, axis, [(source, source + steps) for source in range(count - steps)])


def exchange(value):
    return lax.all_to_all(value, "head", split_axis=0, concat_axis=0, tiled=True)


def after(value, earlier):
    return lax.optimization_barrier((value, earlier))[0]


def pack_kernel(pieces, group, groups, rate_ref, *refs):
    sources = refs[: len(pieces)]
    out_ref, held, came, went = refs[len(pieces) : len(pieces) + 4]
    peers, _, size = out_ref.shape
    rows = held.shape[1]
    inward, outward = [], []
    for d in range(peers):
        at = 0
        for ref, g in zip(sources, pieces):
            for h in range(group):
                n = len(inward)
                column = ((d * groups + g) * group + h) * size
                source = ref.at[:, pl.ds(column, size)]
                inward.append(pltpu.make_async_copy(source, held.at[n], came.at[n]))
                target = out_ref.at[d, pl.ds(at, rows)]
                outward.append(pltpu.make_async_copy(held.at[n], target, went.at[n]))
                at += rows
    for copy in inward:
        copy.start()
    extra = []
    if rate_ref is not None:
        turned, sent = refs[len(pieces) + 4 :]
        heads = rate_ref.shape[0] // peers
        shape = (peers * SUBLANES, rate_ref.shape[0])
        slot = lax.broadcasted_iota(jnp.int32, shape, 0)
        source = lax.broadcasted_iota(jnp.int32, shape, 1)
        chosen = dot(
            (source == slot // SUBLANES * heads + slot % SUBLANES).astype(jnp.bfloat16),
            rate_ref[...],
        )
        turned[:, :, :rows] = chosen.astype(jnp.bfloat16).reshape(peers, SUBLANES, rows)
        for d in range(peers):
            target = out_ref.at[d, pl.ds(at, SUBLANES)]
            extra.append(pltpu.make_async_copy(turned.at[d], target, sent.at[d]))
            extra[-1].start()
    for before, behind in zip(inward, outward):
        before.wait()
        behind.start()
    for copy in outward + extra:
        copy.wait()


def pack(parts, peers, group, groups, size, rates=None):
    rows = parts[0][0].shape[0]
    operands = [array for array, _ in parts]
    pieces = [g for _, g in parts]
    copies = peers * len(parts) * group
    count = len(parts) * group * rows
    specs = [pl.BlockSpec(memory_space=pl.ANY) for _ in parts]
    scratch = [
        pltpu.VMEM((copies, rows, size), jnp.bfloat16),
        pltpu.SemaphoreType.DMA((copies,)),
        pltpu.SemaphoreType.DMA((copies,)),
    ]
    body = functools.partial(pack_kernel, pieces, group, groups)
    if rates is None:
        body = functools.partial(body, None)
    else:
        operands.insert(0, rates)
        specs.insert(0, pl.BlockSpec(memory_space=pltpu.VMEM))
        count += SUBLANES
        scratch += [
            pltpu.VMEM((peers, SUBLANES, size), jnp.bfloat16),
            pltpu.SemaphoreType.DMA((peers,)),
        ]
    return pl.pallas_call(
        body,
        in_specs=specs,
        out_specs=pl.BlockSpec(memory_space=pl.ANY),
        out_shape=jax.ShapeDtypeStruct((peers, count, size), jnp.bfloat16),
        scratch_shapes=scratch,
        compiler_params=PARAMS,
        cost_estimate=cost(0, 4 * peers * count * size),
    )(*operands)


def update_kernel(first_head, k_ref, v_ref, rate_ref, init_ref, out_ref):
    peers, rows, size = k_ref.shape
    head = first_head + pl.program_id(0)
    w_gate, w_up, w_down = init_ref[0, 0], init_ref[1, 0], init_ref[2, 0]
    span = max(1, 512 // rows)
    total = [0.0, 0.0, 0.0]
    for start in range(0, peers, span):
        here = slice(start, start + span)
        tokens = span * rows
        keys = k_ref[here].reshape(tokens, size)
        targets = []
        for s in range(start, start + span):
            turned = jnp.transpose(rate_ref[s].astype(jnp.float32))[:rows]
            lane = lax.broadcasted_iota(jnp.int32, turned.shape, 1)
            rate = jnp.sum(jnp.where(lane == head, turned, 0.0), axis=1, keepdims=True)
            targets.append((rate * v_ref[s].astype(jnp.float32)).astype(jnp.bfloat16))
        targets = jnp.concatenate(targets, axis=0)
        gate_pre = dot_nt(w_gate, keys)
        up_pre = dot_nt(w_up, keys)
        back = dot_nt(w_down, targets)
        sigma = jax.nn.sigmoid(gate_pre)
        gate_act = gate_pre * sigma
        hidden = (gate_act * up_pre).astype(jnp.bfloat16)
        back_gate = (back * up_pre * sigma * (1.0 + gate_pre * (1.0 - sigma))).astype(jnp.bfloat16)
        back_up = (back * gate_act).astype(jnp.bfloat16)
        total[0] += dot(back_gate, keys)
        total[1] += dot(back_up, keys)
        total[2] += dot(hidden, targets)
    for i in range(3):
        out_ref[i, 0] = total[i]


def updates(packed, k_at, v_at, rate_from, fast_init, first_head, group, rows):
    peers, depth, size = rate_from.shape
    hid = fast_init.shape[2]
    length = peers * rows
    block = (peers, rows, size)
    last = depth // SUBLANES - 1
    return pl.pallas_call(
        functools.partial(update_kernel, first_head),
        grid=(group,),
        in_specs=[
            pl.BlockSpec(block, lambda h: (0, k_at + h, 0)),
            pl.BlockSpec(block, lambda h: (0, v_at + h, 0)),
            pl.BlockSpec((peers, SUBLANES, size), lambda h: (0, last, 0)),
            pl.BlockSpec((3, 1, hid, size), lambda h: (0, first_head + h, 0, 0)),
        ],
        out_specs=pl.BlockSpec((3, 1, hid, size), lambda h: (0, h, 0, 0)),
        out_shape=jax.ShapeDtypeStruct((3, group, hid, size), jnp.float32),
        compiler_params=PARAMS,
        cost_estimate=cost(
            group * 6 * 2 * length * size * hid, group * 4 * length * size, group * length * hid
        ),
    )(packed, packed, rate_from, fast_init)


def attend_kernel(place_ref, q_ref, k_ref, v_ref, ek_ref, ev_ref, fit_ref, *refs):
    peers, rows, size = q_ref.shape
    length = peers * rows
    first = place_ref[0] == 0
    factor = size**-0.5 * LOG2E
    tile = min(256, length)
    span = tile // rows
    flat = lambda ref, low, high: ref[low // rows : high // rows].reshape(high - low, size)
    row = lax.broadcasted_iota(jnp.int32, (tile, tile), 0)
    col = lax.broadcasted_iota(jnp.int32, (tile, tile), 1)
    f_gate, f_up, f_down = fit_ref[0, 0], fit_ref[1, 0], fit_ref[2, 0]
    for start in range(0, length, tile):
        stop = start + tile
        query = flat(q_ref, start, stop)
        far = dot_nt(query, flat(ek_ref, start, length))
        near = dot_nt(query, flat(k_ref, 0, stop))
        far_edge = jnp.where(col > row, far[:, :tile], -jnp.inf)
        near_edge = jnp.where(col <= row, near[:, start:], -jnp.inf)
        far_parts = [far_edge] + ([far[:, tile:]] if far.shape[1] > tile else [])
        near_parts = ([near[:, :start]] if start else []) + [near_edge]
        far = jnp.concatenate(far_parts, axis=1)
        near = jnp.concatenate(near_parts, axis=1)
        top_far = jnp.max(far, axis=1, keepdims=True)
        top_near = jnp.max(near, axis=1, keepdims=True)
        top = jnp.where(first, top_near, jnp.maximum(top_near, top_far))
        w_far = jnp.exp2((far - jnp.where(first, jnp.inf, top)) * factor)
        w_near = jnp.exp2((near - top) * factor)
        weight = jnp.sum(w_far, axis=1, keepdims=True) + jnp.sum(w_near, axis=1, keepdims=True)
        attended = dot(w_far.astype(jnp.bfloat16), flat(ev_ref, start, length))
        attended += dot(w_near.astype(jnp.bfloat16), flat(v_ref, 0, stop))
        q_gate = dot_nt(query, f_gate)
        q_up = dot_nt(query, f_up)
        q_hidden = (q_gate * jax.nn.sigmoid(q_gate) * q_up).astype(jnp.bfloat16)
        combined = attended / weight + dot(q_hidden, f_down)
        combined = combined.astype(jnp.bfloat16).reshape(span, rows, size)
        if len(refs) == 1:
            refs[0][start // rows : stop // rows, 0] = combined
        else:
            for n in range(span):
                refs[-1][place_ref[1] ^ (start // rows + n)] = combined[n]
    for step, out_ref in enumerate(refs[:-1]):
        out_ref[0] = refs[-1][step]


def attend(place, q_from, q_at, kv_from, k_at, v_at, edge, ek_at, ev_at, fitted, group, rows, split):
    peers, _, size = q_from.shape
    hid = fitted.shape[2]
    length = peers * rows
    at = lambda start: pl.BlockSpec((peers, rows, size), lambda h: (0, start + h, 0))
    return pl.pallas_call(
        attend_kernel,
        grid=(group,),
        in_specs=[
            pl.BlockSpec(memory_space=pltpu.SMEM),
            at(q_at),
            at(k_at),
            at(v_at),
            at(ek_at),
            at(ev_at),
            pl.BlockSpec((3, 1, hid, size), lambda h: (0, h, 0, 0)),
        ],
        out_specs=[pl.BlockSpec((1, rows, size), lambda h: (h, 0, 0))] * peers
        if split
        else pl.BlockSpec((peers, 1, rows, size), lambda h: (0, h, 0, 0)),
        out_shape=[jax.ShapeDtypeStruct((group, rows, size), jnp.bfloat16)] * peers
        if split
        else jax.ShapeDtypeStruct((peers, group, rows, size), jnp.bfloat16),
        scratch_shapes=[pltpu.VMEM((peers, rows, size), jnp.bfloat16)] if split else [],
        compiler_params=PARAMS,
        cost_estimate=cost(
            group * length * size * 2 * (2 * (WINDOW + 256) + 3 * hid),
            group * 12 * length * size,
            group * length * (WINDOW + 256),
        ),
    )(place, q_from, kv_from, kv_from, edge, edge, fitted)


def swap_order(count):
    short = [step for step in (2, 3) if step < count]
    return short + list(range(count - 1, 3, -1)) + [1, 0]


def swap(pieces):
    count = lax.axis_size("head")
    return [
        lax.ppermute(pieces[step], "head", [(i, i ^ step) for i in range(count)])
        if step
        else pieces[0]
        for step in swap_order(count)
    ]


def norm_kernel(place_ref, first_ref, *refs):
    *pieces, gain_ref, out_ref = refs
    peers, group, rows, size = first_ref.shape
    width = out_ref.shape[1]
    parts = [(lambda p=p, h=h: first_ref[p, h], p * 2 * group + h) for p in range(peers) for h in range(group)]
    for step, ref in zip(swap_order(peers), pieces):
        p = place_ref[1] ^ step
        parts += [(lambda ref=ref, h=h: ref[h], (p * 2 + 1) * group + h) for h in range(group)]
    square = jnp.zeros((rows, size), jnp.float32)
    for load, _ in parts:
        x = load().astype(jnp.float32)
        square += x * x
    factor = lax.rsqrt(jnp.sum(square, axis=1, keepdims=True) / width + EPSILON)
    for load, head in parts:
        here = pl.ds(pl.multiple_of(head * size, size), size)
        x = load().astype(jnp.float32)
        out_ref[:, here] = (x * factor * gain_ref[:, here]).astype(jnp.bfloat16)


def normalize(place, first, pieces, gain):
    peers, group, rows, size = first.shape
    width = gain.shape[0]
    step = min(128, rows)
    return pl.pallas_call(
        norm_kernel,
        grid=(rows // step,),
        in_specs=[
            pl.BlockSpec(memory_space=pltpu.SMEM),
            pl.BlockSpec((peers, group, step, size), lambda i: (0, 0, i, 0)),
        ]
        + [pl.BlockSpec((group, step, size), lambda i: (0, i, 0)) for _ in pieces]
        + [pl.BlockSpec((1, width), lambda i: (0, 0))],
        out_specs=pl.BlockSpec((step, width), lambda i: (i, 0)),
        out_shape=jax.ShapeDtypeStruct((rows, width), jnp.bfloat16),
        compiler_params=PARAMS,
        cost_estimate=cost(5 * rows * width, 4 * rows * width),
    )(place, first, *pieces, gain.reshape(1, width))


def earlier_sum(value, axis, dtype):
    before = jnp.zeros_like(value)
    for step in range(1, lax.axis_size(axis)):
        running = (value + before).astype(dtype)
        before = before + lax.ppermute(running, axis, [(step - 1, step)]).astype(jnp.float32)
    return before


def refit(initial, before):
    initial = initial.astype(jnp.float32)
    target_ms = jnp.mean(initial * initial, axis=3, keepdims=True)
    renewed = initial + before
    current = jnp.mean(renewed * renewed, axis=3, keepdims=True)
    return (renewed * jnp.sqrt(target_ms) * lax.rsqrt(current + EPSILON)).astype(jnp.bfloat16)


def on_device(queries, keys, values, rates, fast_init, gain):
    peers = lax.axis_size("head")
    rows = queries.shape[0]
    heads = fast_init.shape[1]
    size = fast_init.shape[3]
    groups = 2
    group = heads // groups
    place = jnp.stack([lax.axis_index("ctx"), lax.axis_index("head")]).astype(jnp.int32)
    lay = lambda *parts, **more: pack(parts, peers, group, groups, size, **more)

    kv_a = exchange(lay((keys, 0), (values, 0), rates=rates.T))
    kv_a, kvq = lax.optimization_barrier((kv_a, lay((keys, 1), (values, 1), (queries, 0))))
    kvq = exchange(kvq)
    edge_a = from_behind(kv_a, "ctx", 1)
    up_a = updates(kv_a, 0, group, kv_a, fast_init, 0, group, rows)
    fit_a = refit(fast_init[:, :group], earlier_sum(up_a, "ctx", jnp.float32))
    kvq, q_b, fit_a = lax.optimization_barrier((kvq, lay((queries, 1)), fit_a))
    q_b = exchange(q_b)
    kv_b = kvq[:, : 2 * group * rows]
    edge_b = from_behind(kv_b, "ctx", 1)
    up_b = updates(kv_b, 0, group, kv_a, fast_init, group, group, rows)
    fit_b = refit(fast_init[:, group:], earlier_sum(up_b, "ctx", jnp.bfloat16))
    fit_a = after(fit_a, up_b)
    out_a = attend(place, kvq, 2 * group, kv_a, 0, group, edge_a, 0, group, fit_a, group, rows, False)
    back_a = exchange(after(out_a, q_b))
    out_b = attend(place, q_b, 0, kv_b, 0, group, edge_b, 0, group, fit_b, group, rows, True)
    return normalize(place, back_a, swap(out_b), gain)


def solution(mesh):
    rows = P(("ctx", "head"), None)
    in_specs = (rows, rows, rows, rows, P(None, "head", None, None), P())
    return jax.shard_map(on_device, mesh=mesh, in_specs=in_specs, out_specs=rows, check_vma=False)
```
